32 devices in a mesh: blk: 8 (over z, y), lev: 4 (over x, core).
Axes of the slice: x: 2, y: 2, z: 4, core: 2. Of those that a mesh axis runs over, the one named last changes fastest.
Arguments:
- adjoint_in: float32 [512, 12, 1024], P('blk', 'lev'), may hold values from -6 to 6
- courant: float32 [2, 512, 12, 1024], P(None, 'blk', 'lev'), may hold values from 0.05 to 0.45
- mixing: float32 [512, 12, 1024], P('blk', 'lev'), may hold values from 0.5 to 8
- oh_rate: float32 [512, 12, 1024], P('blk', 'lev'), may hold values from 0.02 to 0.6
- substeps: int32 [512], P('blk'), may hold values from 1 to 4
- nest_weight: float32 [512, 128], P('blk'), may hold values from 0.2 to 0.9
- dest_device: int32 [512, 1], P('blk'), may hold values from 0 to 7; in each aligned block of 64 rows (0 to 63, 64 to 127, ...) at most 16 rows name the same one
- dest_slot: int32 [512], P('blk'), may hold values from 0 to 63
- emission_profile: float32 [12], P('lev'), may hold values from 0.05 to 1
- tile_owner: int32 [512], P('blk'), may hold values from 0 to 127, as said below
Outputs:
- adjoint_out: float32 [512, 12, 1024], P('blk', 'lev')
- tile_grad: float32 [128, 1024], P(('blk', 'lev'))
The draws below stay inside these ranges and needn't reach their ends.
Inputs may be any that keep to these rules, and one draw needn't show every extreme that they name: Of the 64 blocks of one index of blk, at most 16 have the same dest_device. Tiles form 8 groups of 16 consecutive tiles. Of the 64 blocks of one index of blk, at most 16 have tile_owner in the same group, and some group holds exactly 16 of them.
All inputs are finite; a program needn't handle non-finite values.
Results may differ from the reference program's by a relative error of at most 0.0003.
Values sent between devices are 32-bit elements; how exact they have to be, the bound alone decides.
A program may use at most 128 MiB of HBM per device.

```python
import math
import jax
import jax.numpy as jnp
import numpy as np

NB_DEV = 64
SIDE = 32
RMAX = 4
STEPS = 2
CELLS = 1024
CYCLE = 128
BLOCKS = 512
LEVELS = 12
CYCLE_PEERS = 8
CAP = 16
TILES = 128


def owner_rows(sub):
    slot_total = CYCLE_PEERS * CAP
    group_size = NB_DEV // 4
    first, second, third, fourth = jax.random.split(sub, 4)
    scores = jax.random.permutation(first, slot_total).astype(jnp.int32)
    full_group = jax.random.randint(second, (), 0, CYCLE_PEERS).astype(jnp.int32)
    slot_ids = jnp.arange(slot_total, dtype=jnp.int32)
    forced = slot_ids // CAP == full_group
    scores = jnp.where(forced, -1 - slot_ids, scores)
    chosen = jnp.argsort(scores, stable=True)[:NB_DEV].astype(jnp.int32)
    chosen = chosen[jax.random.permutation(fourth, NB_DEV)]
    groups = chosen // CAP
    within = jax.random.randint(third, (NB_DEV,), 0, group_size).astype(jnp.int32)
    return groups * group_size + within


def draw_tile_owner(key, part):
    keys_all = jax.random.split(jax.random.fold_in(key, 71), CYCLE_PEERS)
    return jax.vmap(owner_rows)(keys_all).reshape(BLOCKS).astype(jnp.int32)


def place_ends(values, own_key, least, high):
    dims = values.shape
    place = [jax.random.randint(jax.random.fold_in(own_key, axis), (), 0, dims[axis]) for axis in range(len(dims))]
    values = values.at[tuple(place)].set(least)
    longest = dims.index(max(dims))
    place[longest] = (place[longest] + 1) % dims[longest]
    return values.at[tuple(place)].set(high)


def block_scale(own_key, dims, shards, smallest, largest):
    def one(axis_at, parts):
        draws = jax.random.uniform(jax.random.fold_in(jax.random.fold_in(own_key, 6), axis_at), (parts,), jnp.float32, smallest / len(shards), largest / len(shards))
        return jnp.repeat(jnp.exp(draws), dims[axis_at] // parts).reshape((-1,) + (1,) * (len(dims) - axis_at - 1))

    loudness = one(*shards[0])
    for cut in shards[1:]:
        loudness = loudness * one(*cut)
    return loudness


def deal_out(rng, own, number, rows, count, top, bound, skew):
    ranking = jax.random.permutation(rng, count)
    packed, usual = portions_of(count, rows * top, bound, skew, True), portions_of(count, rows * top, bound, skew, False)
    places = jnp.arange(count)

    def named(lengths, rotation):
        used = int((lengths > 0).sum())
        fixed = max(1, used // 4)
        moved = fixed + (places - fixed + rotation * (used - fixed)) % max(1, count - fixed)
        return jnp.zeros((count,), jnp.int32).at[ranking[jnp.where(places < fixed, places, moved)]].set(jnp.asarray(lengths, jnp.int32))

    lengths = jnp.where(number % 4 == 0, named(packed, number // 4), named(usual, number - number // 4 - 1))
    mixed = jax.random.permutation(jax.random.fold_in(own, 3), count)
    giver, sink = mixed[0:count // 2 * 2:2], mixed[1:count // 2 * 2:2]
    room = jnp.minimum(lengths[giver] - 1, bound - lengths[sink]) // 2
    room = jnp.where((giver == ranking[0]) | (sink == ranking[0]) | (lengths[sink] == 0), 0, jnp.maximum(room, 0))
    moved = jax.random.randint(jax.random.fold_in(own, 4), (count // 2,), 0, 1 << 20) % (room + 1)
    lengths = lengths.at[giver].add(-moved).at[sink].add(moved)
    members = jnp.searchsorted(jnp.cumsum(lengths), jnp.arange(rows * top), side="right").astype(jnp.int32)
    table = members.reshape(top, rows).T
    table = table[jax.random.permutation(jax.random.fold_in(own, 1), rows)]
    rotation = jax.random.randint(jax.random.fold_in(own, 2), (rows, 1), 0, top)
    return jnp.take_along_axis(table, (jnp.arange(top)[None, :] + rotation) % top, axis=1)


def portions_of(amount, total, reach, lean, full):
    portions = [(1 << 20) // math.isqrt(standing ** lean) + 1 for standing in range(1, amount + 1)]
    largest = reach if full else min(reach, max(-(-total // amount), total * portions[0] // sum(portions)))
    least = 1 if total - largest >= amount - 1 else 0
    counts, rest = [largest] + [least] * (amount - 1), total - largest - least * (amount - 1)
    while rest > 0:
        free = [i for i in range(1, amount) if counts[i] < largest] or [i for i in range(1, amount) if counts[i] < reach]
        pool, budget = sum([portions[i] for i in free]), rest
        for i in free:
            extra = min(reach - counts[i], max(1, budget * portions[i] // pool), rest)
            counts[i] = counts[i] + extra
            rest = rest - extra
    return np.array(counts)


def scatter_about(stream_key, dims, spread, most, cuts=(), kind=jnp.bfloat16):
    array = jax.random.normal(stream_key, dims, jnp.float32) * spread
    if len(cuts) > 0:
        array = block_scale(stream_key, dims, cuts, -0.22, 0.18) * array
    return jnp.clip(array, min=-most, max=most).astype(kind)


def setup_inputs(seed: int = 0) -> dict:
    key_list = jax.random.split(jax.random.key(seed), 11)
    adjoint_in = scatter_about(key_list[0], (BLOCKS, LEVELS, CELLS), 1.0, 6.0, ((0, 8), (1, 4)), jnp.float32)
    courant = jnp.clip(0.05 + 0.39999999 * jax.random.uniform(key_list[1], (2, BLOCKS, LEVELS, CELLS), jnp.float32) ** block_scale(key_list[1], (2, BLOCKS, LEVELS, CELLS), ((1, 8), (2, 4)), -0.2, 0.2), 0.05, 0.45)
    mixing = jnp.clip(jnp.exp(math.log(8.0) - 2.7725887 * jax.random.uniform(key_list[2], (BLOCKS, LEVELS, CELLS), jnp.float32) ** block_scale(key_list[2], (BLOCKS, LEVELS, CELLS), ((0, 8), (1, 4)), -0.2, 0.2)), 0.5, 8.0)
    oh_rate = jnp.clip(jnp.exp(math.log(0.6) - 3.4011974 * jax.random.uniform(key_list[3], (BLOCKS, LEVELS, CELLS), jnp.float32) ** block_scale(key_list[3], (BLOCKS, LEVELS, CELLS), ((0, 8), (1, 4)), -0.2, 0.2)), 0.02, 0.6)
    substeps = place_ends(jax.random.randint(key_list[4], (BLOCKS,), 1, RMAX + 1), jax.random.fold_in(key_list[4], 1), 1, RMAX).astype(jnp.int32)
    nest_weight = jnp.clip(0.2 + 0.7 * jax.random.uniform(key_list[5], (BLOCKS, CYCLE), jnp.float32) ** block_scale(key_list[5], (BLOCKS, CYCLE), ((0, 8),), -0.2, 0.2), 0.2, 0.9)
    dest_device_keys = jax.random.split(jax.random.fold_in(key_list[6], 1), BLOCKS // NB_DEV)
    dest_device_turns = jax.random.permutation(jax.random.fold_in(key_list[6], 3), BLOCKS // NB_DEV)
    dest_device = jax.vmap(lambda own, number: deal_out(jax.random.fold_in(key_list[6], 2), own, number, NB_DEV, CYCLE_PEERS, 1, CAP, 2))(dest_device_keys, dest_device_turns).reshape((BLOCKS, 1))
    dest_slot = place_ends(jax.random.randint(key_list[7], (BLOCKS,), 0, NB_DEV), jax.random.fold_in(key_list[7], 1), 0, NB_DEV - 1).astype(jnp.int32)
    emission_profile = jnp.clip(jnp.exp(math.log(1.0) - 2.9957323 * jax.random.uniform(key_list[8], (LEVELS,), jnp.float32) ** block_scale(key_list[8], (LEVELS,), ((0, 4),), -0.2, 0.2)), 0.05, 1.0)
    tile_owner = draw_tile_owner(jax.random.fold_in(key_list[10], 71), 0)
    return {"adjoint_in": adjoint_in, "courant": courant, "mixing": mixing, "oh_rate": oh_rate, "substeps": substeps, "nest_weight": nest_weight, "dest_device": dest_device, "dest_slot": dest_slot, "emission_profile": emission_profile, "tile_owner": tile_owner}


def solve_columns(right_side, coupling):
    level_count = right_side.shape[1]
    ratios = []
    scaled = []
    for level in range(level_count):
        lower_k = coupling[:, level - 1] if level > 0 else 0.0
        upper_k = coupling[:, level] if level < level_count - 1 else 0.0
        diag_term = 1.0 + lower_k + upper_k
        if level == 0:
            pivot_val = diag_term
            scaled.append(right_side[:, 0] / pivot_val)
        else:
            pivot_val = diag_term + lower_k * ratios[level - 1]
            scaled.append((right_side[:, level] + lower_k * scaled[level - 1]) / pivot_val)
        ratios.append(-upper_k / pivot_val)
    solved = [None] * level_count
    solved[level_count - 1] = scaled[level_count - 1]
    for level in range(level_count - 2, -1, -1):
        solved[level] = scaled[level] - ratios[level] * solved[level + 1]
    return jnp.stack(solved, axis=1)


def stencil(adjoint, east_u, north_u, side_len):
    shape_grid = adjoint.shape[:-1] + (side_len, side_len)
    grid_view = adjoint.reshape(shape_grid)
    east_c = east_u.reshape(shape_grid)
    north_c = north_u.reshape(shape_grid)
    zero_col = jnp.zeros(shape_grid[:-1] + (1,), jnp.float32)
    east_adj = jnp.concatenate([grid_view[..., 1:], zero_col], axis=-1)
    zero_row = jnp.zeros(shape_grid[:-2] + (1, side_len), jnp.float32)
    north_adj = jnp.concatenate([grid_view[..., 1:, :], zero_row], axis=-2)
    result = (1.0 - east_c - north_c) * grid_view + east_c * east_adj + north_c * north_adj
    return result.reshape(adjoint.shape)


def faces(adjoint, side_len):
    grid_view = adjoint.reshape(adjoint.shape[:-1] + (side_len, side_len))
    return jnp.concatenate([grid_view[..., 0, :], grid_view[..., side_len - 1, :], grid_view[..., :, 0], grid_view[..., :, side_len - 1]], axis=-1)


def add_faces(adjoint, arrivals, side_len):
    grid_view = adjoint.reshape(adjoint.shape[:-1] + (side_len, side_len))
    grid_view = grid_view.at[..., 0, :].add(arrivals[..., 0:side_len])
    grid_view = grid_view.at[..., side_len - 1, :].add(arrivals[..., side_len:2 * side_len])
    grid_view = grid_view.at[..., :, 0].add(arrivals[..., 2 * side_len:3 * side_len])
    grid_view = grid_view.at[..., :, side_len - 1].add(arrivals[..., 3 * side_len:])
    return grid_view.reshape(adjoint.shape)


def reference(adjoint_in, courant, mixing, oh_rate, substeps, nest_weight, dest_device, dest_slot, emission_profile, tile_owner):
    side_len = SIDE
    survive = jnp.exp(-oh_rate)
    target = (dest_device[:, 0] * NB_DEV + dest_slot).astype(jnp.int32)
    adjoint = adjoint_in
    grad_sum = jnp.zeros((BLOCKS, CELLS), jnp.float32)
    for step_index in range(STEPS):
        grad_sum = grad_sum + jnp.sum(adjoint * emission_profile[None, :, None], axis=1)
        adjoint = solve_columns(adjoint * survive, mixing)
        cycle_out = faces(adjoint, side_len) * nest_weight[:, None, :]
        arrivals = jax.ops.segment_sum(cycle_out, target, num_segments=BLOCKS)
        advected = adjoint
        for substep in range(RMAX):
            active = (substep < substeps)[:, None, None]
            advected = jnp.where(active, stencil(advected, courant[0], courant[1], side_len), advected)
        adjoint = add_faces(advected, arrivals, side_len)
    tile_grad = jax.ops.segment_sum(grad_sum, tile_owner, num_segments=TILES)
    return adjoint, tile_grad
```

```python
import functools

import jax
import jax.numpy as jnp
from jax import lax
from jax.experimental import pallas as pl
from jax.experimental.pallas import tpu as pltpu
from jax.sharding import PartitionSpec as P

RMAX = 4
STEPS = 2
CHUNKS = 4
GROUP = 8
MESH = pl.DeviceIdType.MESH
F32 = jnp.float32
BF16 = jnp.bfloat16


def split_dot(left, right, dims=((1,), (0,))):
    def run(a, b):
        return lax.dot_general(a, b, (dims, ((), ())), preferred_element_type=F32)

    if left.dtype == BF16:
        high = right.astype(BF16)
        low = (right - high.astype(F32)).astype(BF16)
        return run(left, high) + run(left, low)
    high = left.astype(BF16)
    low = (left - high.astype(F32)).astype(BF16)
    return run(high, right) + run(low, right)


def each(count, body):
    if count <= 16:
        for off in range(1, count):
            body(off)
    else:
        lax.fori_loop(1, count, lambda off, c: (body(off), c)[1], 0)


def kernel(
    peers,
    levs,
    adj,
    courant,
    mix,
    oh,
    ints,
    weight,
    profile,
    out,
    tile_out,
    surv,
    centre,
    east,
    north,
    x,
    coef,
    middle,
    grad,
    gather_t,
    spread_t,
    pick,
    place,
    flat,
    key_send,
    key_recv,
    face_send,
    face_recv,
    line_send,
    line_recv,
    cross_send,
    cross_recv,
    back_send,
    back_recv,
    tiles,
    tiles_recv,
    owned,
    owned_recv,
    line_ss,
    line_rs,
    cross_ss,
    cross_rs,
    back_ss,
    back_rs,
    key_ss,
    key_rs,
    face_ss,
    face_rs,
    tile_ss,
    tile_rs,
    own_ss,
    own_rs,
):
    lev_here, blocks, cells = adj.shape
    cycle = weight.shape[1]
    side = cycle // 4
    cap = key_send.shape[1]
    slots = peers * cap
    chunk = blocks // CHUNKS
    my_blk = lax.axis_index("blk")
    my_lev = lax.axis_index("lev")
    lower = my_lev < 2
    outer = jnp.logical_or(my_lev == 0, my_lev == levs - 1)

    def peer_at(off):
        return lax.rem(my_blk + off, peers)

    def source_at(off):
        return lax.rem(my_blk + peers - off, peers)

    barrier = pltpu.get_barrier_semaphore()
    each(peers, lambda off: pl.semaphore_signal(
        barrier, inc=1, device_id=(peer_at(off), my_lev), device_id_type=MESH))
    for off in range(1, levs):
        pl.semaphore_signal(
            barrier, inc=1, device_id=(my_blk, lax.rem(my_lev + off, levs)), device_id_type=MESH)

    def rows_of(part, item):
        return pl.ds(pl.multiple_of(part * chunk + item * GROUP, GROUP), GROUP)

    def level_at(p):
        return jnp.where(lower, p, lev_here - 1 - p)

    def link_at(p):
        return jnp.where(lower, p, lev_here - 2 - p)

    def link_pair(d, k, flag):
        inv = 1.0 / (d + k)
        return jnp.where(flag, inv, 0.0), jnp.where(flag, k * inv, 1.0)

    last = lev_here - 1

    def line_copy(step, part, target):
        return pltpu.make_async_remote_copy(
            line_send.at[step, part], line_recv.at[step, part],
            line_ss.at[step, part], line_rs.at[step, part],
            device_id=(my_blk, target), device_id_type=MESH)

    def first_line(part, target):
        return pltpu.make_async_remote_copy(
            line_send.at[STEPS, part], line_recv.at[STEPS, part],
            line_ss.at[STEPS, part], line_rs.at[STEPS, part],
            device_id=(my_blk, target), device_id_type=MESH)

    def cross_copy(step, part, target):
        return pltpu.make_async_remote_copy(
            cross_send.at[step, part], cross_recv.at[step, part],
            cross_ss.at[step, part], cross_rs.at[step, part],
            device_id=(my_blk, target), device_id_type=MESH)

    def back_copy(step, part, target):
        return pltpu.make_async_remote_copy(
            back_send.at[step, part], back_recv.at[step, part],
            back_ss.at[step, part], back_rs.at[step, part],
            device_id=(my_blk, target), device_id_type=MESH)

    partner = jnp.where(lower, 1 - my_lev, 5 - my_lev)
    across = 3 - my_lev

    def forward(step, rows, d, f):
        for p in range(lev_here):
            if p > 0:
                c = coef[2 * (p - 1), rows, :]
                f = x[level_at(p), rows, :] * surv[level_at(p), rows, :] + c * f
            x[level_at(p), rows, :] = f
            if step == 0:
                if p > 0:
                    d = 1.0 + c * d
                if p < last:
                    k = mix[link_at(p), rows, :]
                    inv = 1.0 / (d + k)
                    coef[2 * p, rows, :] = k * inv
                    coef[2 * p + 1, rows, :] = inv
        return d, f

    def backward(rows, value):
        x[level_at(last), rows, :] = value
        for p in range(last - 1, -1, -1):
            value = x[level_at(p), rows, :] * coef[2 * p + 1, rows, :] + coef[2 * p, rows, :] * value
            x[level_at(p), rows, :] = value
        return value

    items = chunk // GROUP
    end_c, end_i = 2 * last, 2 * last + 1

    def send_rows(item):
        return pl.ds(pl.multiple_of(item * GROUP, GROUP), GROUP)

    def solve(step):
        @pl.when(outer)
        def _():
            for part in range(CHUNKS):
                @pl.loop(0, items)
                def _(item):
                    rows, own = rows_of(part, item), send_rows(item)
                    d, f = forward(
                        step, rows, jnp.ones((GROUP, cells), F32),
                        x[level_at(0), rows, :] * surv[level_at(0), rows, :])
                    if step == 0:
                        inv, c = link_pair(d, mix[last, rows, :], lower)
                        coef[end_c, rows, :] = c
                        coef[end_i, rows, :] = inv
                        line_send[STEPS, part, own, :] = c * d
                    else:
                        c = coef[end_c, rows, :]
                    line_send[step, part, own, :] = c * f

                if step == 0:
                    first_line(part, partner).start()
                line_copy(step, part, partner).start()
            for part in range(CHUNKS):
                back_copy(step, part, partner).wait_recv()

                @pl.loop(0, items)
                def _(item):
                    rows, own = rows_of(part, item), send_rows(item)
                    value = x[level_at(last), rows, :] * coef[end_i, rows, :]
                    value = value + coef[end_c, rows, :] * back_recv[step, part, own, :]
                    backward(rows, value)

        @pl.when(jnp.logical_not(outer))
        def _():
            for part in range(CHUNKS):
                if step == 0:
                    first_line(part, partner).wait_recv()
                line_copy(step, part, partner).wait_recv()

                @pl.loop(0, items)
                def _(item):
                    rows, own = rows_of(part, item), send_rows(item)
                    f_in = line_recv[step, part, own, :]
                    d = None
                    if step == 0:
                        d_in = line_recv[STEPS, part, own, :]
                        inv, c_in = link_pair(
                            d_in, mix[last, rows, :], jnp.logical_not(lower))
                        middle[0, rows, :] = inv
                        middle[1, rows, :] = c_in
                        d = 1.0 + c_in * d_in
                    else:
                        c_in = middle[1, rows, :]
                    d, f = forward(
                        step, rows, d,
                        x[level_at(0), rows, :] * surv[level_at(0), rows, :] + c_in * f_in)
                    if step == 0:
                        _, c = link_pair(d, mix[last, rows, :], lower)
                        coef[end_c, rows, :] = c
                        coef[end_i, rows, :] = d
                        cross_send[STEPS, part, own, :] = c * d
                    else:
                        c = coef[end_c, rows, :]
                    cross_send[step, part, own, :] = c * f

                if step == 0:
                    cross_copy(STEPS, part, across).start()
                cross_copy(step, part, across).start()
            for part in range(CHUNKS):
                if step == 0:
                    cross_copy(STEPS, part, across).wait_recv()
                cross_copy(step, part, across).wait_recv()

                @pl.loop(0, items)
                def _(item):
                    rows, own = rows_of(part, item), send_rows(item)
                    if step == 0:
                        d_in = cross_recv[STEPS, part, own, :]
                        _, c_in = link_pair(d_in, mix[last, rows, :], lower)
                        inv = 1.0 / (coef[end_i, rows, :] + c_in * d_in)
                        middle[2, rows, :] = c_in
                        middle[3, rows, :] = inv
                    else:
                        c_in = middle[2, rows, :]
                        inv = middle[3, rows, :]
                    value = (x[level_at(last), rows, :] + c_in * cross_recv[step, part, own, :]) * inv
                    value = backward(rows, value)
                    back_send[step, part, own, :] = (
                        middle[0, rows, :] * line_recv[step, part, own, :]
                        + middle[1, rows, :] * value)

                back_copy(step, part, partner).start()

    def finish_solve(step):
        @pl.when(outer)
        def _():
            for part in range(CHUNKS):
                if step == 0:
                    first_line(part, partner).wait_send()
                line_copy(step, part, partner).wait_send()

        @pl.when(jnp.logical_not(outer))
        def _():
            for part in range(CHUNKS):
                if step == 0:
                    cross_copy(STEPS, part, across).wait_send()
                cross_copy(step, part, across).wait_send()
                back_copy(step, part, partner).wait_send()

    def key_copy(off, whose):
        return pltpu.make_async_remote_copy(
            key_send.at[peer_at(off)], key_recv.at[whose], key_ss.at[off], key_rs.at[off],
            device_id=(peer_at(off), my_lev), device_id_type=MESH)

    def face_copy(step, off, whose):
        return pltpu.make_async_remote_copy(
            face_send.at[step, peer_at(off)], face_recv.at[step, whose],
            face_ss.at[step, off], face_rs.at[step, off],
            device_id=(peer_at(off), my_lev), device_id_type=MESH)

    def tile_copy(off, whose):
        target = lax.rem(my_lev + off, levs)
        return pltpu.make_async_remote_copy(
            tiles.at[target], tiles_recv.at[whose], tile_ss.at[off], tile_rs.at[off],
            device_id=(my_blk, target), device_id_type=MESH)

    def own_copy(off, whose):
        return pltpu.make_async_remote_copy(
            owned.at[peer_at(off)], owned_recv.at[whose], own_ss.at[off], own_rs.at[off],
            device_id=(peer_at(off), my_lev), device_id_type=MESH)

    def split_rows(value, target):
        width = value.shape[1]
        if cap % 8 == 0:
            target[...] = value.reshape(peers, cap, width)
        else:
            flat[:, :width] = value
            for p in range(peers):
                target[p] = flat[p * cap : (p + 1) * cap, :width]

    def join_rows(source):
        width = source.shape[-1]
        if cap % 8 == 0:
            return source[...].reshape(slots, width)
        for p in range(peers):
            flat[p * cap : (p + 1) * cap, :width] = source[p]
        return flat[:, :width]

    @pl.loop(0, blocks // GROUP)
    def _(item):
        rows = pl.ds(pl.multiple_of(item * GROUP, GROUP), GROUP)
        for level in range(lev_here):
            surv[level, rows, :] = jnp.exp(-oh[level, rows, :])
            x[level, rows, :] = adj[level, rows, :]

    pl.semaphore_wait(barrier, peers - 1 + levs - 1)

    def prepare():
        eye = (
            lax.broadcasted_iota(jnp.int32, (blocks, blocks), 0)
            == lax.broadcasted_iota(jnp.int32, (blocks, blocks), 1)
        )

        def column(row):
            return jnp.sum(jnp.where(eye, row, 0.0), axis=1, keepdims=True)

        dest = ints[1:2, :]
        same = jnp.logical_and(
            column(dest) == dest,
            lax.broadcasted_iota(jnp.int32, (blocks, blocks), 0)
            < lax.broadcasted_iota(jnp.int32, (blocks, blocks), 1),
        )
        rank = jnp.sum(jnp.where(same, 1.0, 0.0), axis=0, keepdims=True)
        slot_row = dest * cap + rank
        slot_id = lax.broadcasted_iota(jnp.int32, (slots, blocks), 0).astype(F32)
        pick[...] = jnp.where(slot_id == slot_row, 1.0, 0.0).astype(BF16)
        keys = column(ints[2:3, :]) + jnp.zeros((blocks, 128), F32)
        split_rows(
            jnp.dot(pick[...], keys.astype(BF16), preferred_element_type=F32), key_send)
        key_recv[my_blk] = key_send[my_blk]
        each(peers, lambda off: key_copy(off, my_blk).start())

        face = lax.broadcasted_iota(jnp.int32, (cycle, cells), 0)
        cell = lax.broadcasted_iota(jnp.int32, (cycle, cells), 1)
        wanted = jnp.where(
            face < side, face,
            jnp.where(
                face < 2 * side, face + (cells - 2 * side),
                jnp.where(
                    face < 3 * side, (face - 2 * side) * side,
                    (face - 3 * side) * side + side - 1)))
        spread_t[...] = jnp.where(cell == wanted, 1.0, 0.0).astype(BF16)
        face = lax.broadcasted_iota(jnp.int32, (cells, cycle), 1)
        cell = lax.broadcasted_iota(jnp.int32, (cells, cycle), 0)
        wanted = jnp.where(
            face < side, face,
            jnp.where(
                face < 2 * side, face + (cells - 2 * side),
                jnp.where(
                    face < 3 * side, (face - 2 * side) * side,
                    (face - 3 * side) * side + side - 1)))
        gather_t[...] = jnp.where(cell == wanted, 1.0, 0.0).astype(BF16)

        @pl.loop(0, blocks // GROUP)
        def _(item):
            rows = pl.ds(pl.multiple_of(item * GROUP, GROUP), GROUP)
            cell = lax.broadcasted_iota(jnp.int32, (GROUP, cells), 1)
            total = jnp.zeros((GROUP, cells), F32)
            for level in range(lev_here):
                e, n = courant[0, level, rows, :], courant[1, level, rows, :]
                centre[level, rows, :] = 1.0 - e - n
                east[level, rows, :] = jnp.where(cell % side == side - 1, 0.0, e)
                north[level, rows, :] = jnp.where(cell >= cells - side, 0.0, n)
                total = total + profile[level] * adj[level, rows, :]
            grad[rows, :] = total

        return column(ints[0:1, :])

    solve(0)
    sub_column = prepare()
    sub_wide = sub_column + jnp.zeros((blocks, 128), F32)
    place_ready = False
    flat_sub = sub_wide

    for step in range(STEPS):
        if step > 0:
            solve(step)
        cyc = [
            split_dot(x[level], gather_t[...]) * weight[...] for level in range(lev_here)
        ]
        split_rows(
            split_dot(pick[...], jnp.concatenate(cyc, axis=1)), face_send.at[step])
        face_recv[step, my_blk] = face_send[step, my_blk]
        each(peers, lambda off: face_copy(step, off, my_blk).start())

        if step == STEPS - 1:
            owner = ints[3:4, :].astype(jnp.int32)
            group = owner // (4 * levs)
            row = (owner // 4) % levs * (4 * peers) + group * 4 + owner % 4
            ids = lax.broadcasted_iota(jnp.int32, (4 * peers * levs, blocks), 0)
            hot = jnp.where(ids == row, 1.0, 0.0).astype(BF16)
            tiles[...] = split_dot(hot, grad[...]).reshape(levs, 4 * peers, cells)
            for off in range(1, levs):
                tile_copy(off, my_lev).start()

        for group in range(blocks // GROUP):
            rows = slice(group * GROUP, (group + 1) * GROUP)
            active = flat_sub[rows, 0:1]

            @pl.loop(0, lev_here)
            def _(level):
                value = x[level, rows, :]
                c0, ce, cn = centre[level, rows, :], east[level, rows, :], north[level, rows, :]
                for substep in range(RMAX):
                    moved = (
                        c0 * value
                        + ce * pltpu.roll(value, cells - 1, 1)
                        + cn * pltpu.roll(value, cells - side, 1))
                    value = jnp.where(active > substep, moved, value)
                x[level, rows, :] = value

        if step == 0:
            each(peers, lambda off: key_copy(off, source_at(off)).wait_recv())
            keys = join_rows(key_recv)
            lane = lax.broadcasted_iota(jnp.int32, (slots, 128), 1).astype(F32)
            place[...] = jnp.where(keys == lane, 1.0, 0.0).T[:blocks].astype(BF16)
        else:
            for off in range(1, levs):
                tile_copy(off, lax.rem(my_lev + levs - off, levs)).wait_recv()
            total = tiles[my_lev]
            for off in range(1, levs):
                total = total + tiles_recv[lax.rem(my_lev + levs - off, levs)]
            for p in range(peers):
                owned[p] = total[4 * p : 4 * p + 4]
            each(peers, lambda off: own_copy(off, my_blk).start())
        each(peers, lambda off: face_copy(step, off, source_at(off)).wait_recv())
        arrived = split_dot(place[...], join_rows(face_recv.at[step]))
        for level in range(lev_here):
            value = x[level] + split_dot(
                arrived[:, level * cycle : (level + 1) * cycle], spread_t[...])
            if step < STEPS - 1:
                x[level] = value
                grad[...] = grad[...] + profile[level] * value
            else:
                out[level] = value

    each(peers, lambda off: own_copy(off, source_at(off)).wait_recv())
    tile_out[...] = owned[my_blk]

    def add_owned(off):
        tile_out[...] = tile_out[...] + owned_recv[source_at(off)]

    each(peers, add_owned)
    for step in range(STEPS):
        finish_solve(step)
        each(peers, lambda off: face_copy(step, off, my_blk).wait_send())
    each(peers, lambda off: key_copy(off, my_blk).wait_send())
    for off in range(1, levs):
        tile_copy(off, my_lev).wait_send()
    each(peers, lambda off: own_copy(off, my_blk).wait_send())


def local(
    adjoint_in,
    courant,
    mixing,
    oh_rate,
    substeps,
    nest_weight,
    dest_device,
    dest_slot,
    emission_profile,
    tile_owner,
):
    blocks, lev_here, cells = adjoint_in.shape
    cycle = nest_weight.shape[1]
    peers = lax.axis_size("blk")
    levs = lax.axis_size("lev")
    cap = min(blocks, 2 * blocks // peers)
    chunk = blocks // CHUNKS
    ints = jnp.stack([substeps, dest_device[:, 0], dest_slot, tile_owner]).astype(F32)
    vmem = pl.BlockSpec(memory_space=pltpu.VMEM)
    whole = pltpu.VMEM((lev_here, blocks, cells), F32)
    line = pltpu.VMEM((STEPS + 1, CHUNKS, chunk, cells), F32)
    dma = pltpu.SemaphoreType.DMA
    out, tile_grad = pl.pallas_call(
        functools.partial(kernel, peers, levs),
        out_shape=(
            jax.ShapeDtypeStruct((lev_here, blocks, cells), F32),
            jax.ShapeDtypeStruct((4, cells), F32),
        ),
        in_specs=[vmem] * 6 + [pl.BlockSpec(memory_space=pltpu.SMEM)],
        out_specs=(vmem, vmem),
        scratch_shapes=[
            whole,
            whole,
            whole,
            whole,
            whole,
            pltpu.VMEM((2 * lev_here, blocks, cells), F32),
            pltpu.VMEM((4, blocks, cells), F32),
            pltpu.VMEM((blocks, cells), F32),
            pltpu.VMEM((cells, cycle), BF16),
            pltpu.VMEM((cycle, cells), BF16),
            pltpu.VMEM((peers * cap, blocks), BF16),
            pltpu.VMEM((blocks, peers * cap), BF16),
            pltpu.VMEM((peers * cap, lev_here * cycle), F32),
            pltpu.VMEM((peers, cap, 128), F32),
            pltpu.VMEM((peers, cap, 128), F32),
            pltpu.VMEM((STEPS, peers, cap, lev_here * cycle), F32),
            pltpu.VMEM((STEPS, peers, cap, lev_here * cycle), F32),
            line,
            line,
            line,
            line,
            line,
            line,
            pltpu.VMEM((levs, 4 * peers, cells), F32),
            pltpu.VMEM((levs, 4 * peers, cells), F32),
            pltpu.VMEM((peers, 4, cells), F32),
            pltpu.VMEM((peers, 4, cells), F32),
            dma((STEPS + 1, CHUNKS)),
            dma((STEPS + 1, CHUNKS)),
            dma((STEPS + 1, CHUNKS)),
            dma((STEPS + 1, CHUNKS)),
            dma((STEPS, CHUNKS)),
            dma((STEPS, CHUNKS)),
            dma((peers,)),
            dma((peers,)),
            dma((STEPS, peers)),
            dma((STEPS, peers)),
            dma((levs,)),
            dma((levs,)),
            dma((peers,)),
            dma((peers,)),
        ],
        compiler_params=pltpu.CompilerParams(
            collective_id=0, has_side_effects=True, vmem_limit_bytes=56 * 1024 * 1024
        ),
    )(
        jnp.transpose(adjoint_in, (1, 0, 2)),
        jnp.transpose(courant, (0, 2, 1, 3)),
        jnp.transpose(mixing, (1, 0, 2)),
        jnp.transpose(oh_rate, (1, 0, 2)),
        ints,
        nest_weight,
        emission_profile,
    )
    return jnp.transpose(out, (1, 0, 2)), tile_grad


def solution(mesh):
    placed = (
        P("blk", "lev", None),
        P(None, "blk", "lev", None),
        P("blk", "lev", None),
        P("blk", "lev", None),
        P("blk"),
        P("blk", None),
        P("blk", None),
        P("blk"),
        P("lev"),
        P("blk"),
    )
    return jax.shard_map(
        local,
        mesh=mesh,
        in_specs=placed,
        out_specs=(P("blk", "lev", None), P(("blk", "lev"), None)),
        check_vma=False,
    )
```

```python
import functools

import jax
import jax.numpy as jnp
from jax import lax
from jax.experimental import pallas as pl
from jax.experimental.pallas import tpu as pltpu
from jax.sharding import PartitionSpec as P

RMAX = 4
STEPS = 2
CHUNKS = 4
GROUP = 16
MESH = pl.DeviceIdType.MESH
F32 = jnp.float32
BF16 = jnp.bfloat16


def split_dot(left, right, dims=((1,), (0,))):
    def run(a, b):
        return lax.dot_general(a, b, (dims, ((), ())), preferred_element_type=F32)

    if left.dtype == BF16:
        high = right.astype(BF16)
        low = (right - high.astype(F32)).astype(BF16)
        return run(left, high) + run(left, low)
    rows = left.shape[0]
    high = left.astype(BF16)
    low = (left - high.astype(F32)).astype(BF16)
    both = run(jnp.concatenate([high, low], axis=0), right)
    return both[:rows] + both[rows:]


def each(count, body):
    if count <= 16:
        for off in range(1, count):
            body(off)
    else:
        lax.fori_loop(1, count, lambda off, c: (body(off), c)[1], 0)


def kernel(
    peers,
    levs,
    adj_far,
    courant,
    mix_far,
    oh_far,
    substeps,
    dest_device,
    dest_slot,
    tile_owner,
    weight,
    profile,
    out,
    tile_out,
    surv,
    adj,
    mix,
    oh,
    courant_here,
    load_sems,
    store_sems,
    sub_wide,
    centre,
    east,
    north,
    x,
    coef,
    middle,
    grad,
    gather_t,
    spread_t,
    pick,
    place,
    flat,
    key_send,
    key_recv,
    face_send,
    face_recv,
    line_send,
    line_recv,
    cross_send,
    cross_recv,
    back_send,
    back_recv,
    tiles,
    tiles_recv,
    owned,
    owned_recv,
    line_ss,
    line_rs,
    cross_ss,
    cross_rs,
    back_ss,
    back_rs,
    key_ss,
    key_rs,
    face_ss,
    face_rs,
    tile_ss,
    tile_rs,
    own_ss,
    own_rs,
):
    lev_here, blocks, cells = adj_far.shape
    cycle = weight.shape[1]
    side = cycle // 4
    cap = key_send.shape[1]
    slots = peers * cap
    chunk = blocks // CHUNKS
    my_blk = lax.axis_index("blk")
    my_lev = lax.axis_index("lev")
    lower = my_lev < 2
    outer = jnp.logical_or(my_lev == 0, my_lev == levs - 1)

    def peer_at(off):
        return lax.rem(my_blk + off, peers)

    def source_at(off):
        return lax.rem(my_blk + peers - off, peers)

    loads = [
        pltpu.make_async_copy(source, target, load_sems.at[n])
        for n, (source, target) in enumerate(
            [(oh_far, oh), (adj_far, adj), (mix_far, mix), (courant, courant_here)])
    ]
    fetch = loads[-1]
    for load in loads:
        load.start()
    barrier = pltpu.get_barrier_semaphore()
    each(peers, lambda off: pl.semaphore_signal(
        barrier, inc=1, device_id=(peer_at(off), my_lev), device_id_type=MESH))
    for off in range(1, levs):
        pl.semaphore_signal(
            barrier, inc=1, device_id=(my_blk, lax.rem(my_lev + off, levs)), device_id_type=MESH)

    def rows_of(part, item):
        return pl.ds(pl.multiple_of(part * chunk + item * GROUP, GROUP), GROUP)

    def level_at(p):
        return jnp.where(lower, p, lev_here - 1 - p)

    def link_at(p):
        return jnp.where(lower, p, lev_here - 2 - p)

    def link_pair(d, k, flag):
        inv = 1.0 / (d + k)
        return jnp.where(flag, inv, 0.0), jnp.where(flag, k * inv, 1.0)

    last = lev_here - 1

    def line_copy(step, part, target):
        return pltpu.make_async_remote_copy(
            line_send.at[step, part], line_recv.at[step, part],
            line_ss.at[step, part], line_rs.at[step, part],
            device_id=(my_blk, target), device_id_type=MESH)

    def first_line(part, target):
        return pltpu.make_async_remote_copy(
            line_send.at[STEPS, part], line_recv.at[STEPS, part],
            line_ss.at[STEPS, part], line_rs.at[STEPS, part],
            device_id=(my_blk, target), device_id_type=MESH)

    def cross_copy(step, part, target):
        return pltpu.make_async_remote_copy(
            cross_send.at[step, part], cross_recv.at[step, part],
            cross_ss.at[step, part], cross_rs.at[step, part],
            device_id=(my_blk, target), device_id_type=MESH)

    def back_copy(step, part, target):
        return pltpu.make_async_remote_copy(
            back_send.at[step, part], back_recv.at[step, part],
            back_ss.at[step, part], back_rs.at[step, part],
            device_id=(my_blk, target), device_id_type=MESH)

    partner = jnp.where(lower, 1 - my_lev, 5 - my_lev)
    across = 3 - my_lev

    def forward(step, rows, d, f):
        for p in range(lev_here):
            if p > 0:
                c = coef[2 * (p - 1), rows, :]
                f = x[level_at(p), rows, :] * surv[level_at(p), rows, :] + c * f
            x[level_at(p), rows, :] = f
            if step == 0:
                if p > 0:
                    d = 1.0 + c * d
                if p < last:
                    k = mix[link_at(p), rows, :]
                    inv = 1.0 / (d + k)
                    coef[2 * p, rows, :] = k * inv
                    coef[2 * p + 1, rows, :] = inv
        return d, f

    def backward(rows, value):
        x[level_at(last), rows, :] = value
        for p in range(last - 1, -1, -1):
            value = x[level_at(p), rows, :] * coef[2 * p + 1, rows, :] + coef[2 * p, rows, :] * value
            x[level_at(p), rows, :] = value
        return value

    items = chunk // GROUP
    end_c, end_i = 2 * last, 2 * last + 1

    def send_rows(item):
        return pl.ds(pl.multiple_of(item * GROUP, GROUP), GROUP)

    def key_copy(off, whose):
        return pltpu.make_async_remote_copy(
            key_send.at[peer_at(off)], key_recv.at[whose], key_ss.at[off], key_rs.at[off],
            device_id=(peer_at(off), my_lev), device_id_type=MESH)

    def face_copy(step, off, whose):
        return pltpu.make_async_remote_copy(
            face_send.at[step, peer_at(off)], face_recv.at[step, whose],
            face_ss.at[step, off], face_rs.at[step, off],
            device_id=(peer_at(off), my_lev), device_id_type=MESH)

    def pair_copy(which, target):
        return pltpu.make_async_remote_copy(
            tiles.at[target], tiles_recv.at[which], tile_ss.at[which], tile_rs.at[which],
            device_id=(my_blk, partner), device_id_type=MESH)

    def pair_copies():
        return [pair_copy(0, partner), pair_copy(1, levs - 1 - partner)]

    def far_copy():
        return pltpu.make_async_remote_copy(
            tiles.at[across], tiles_recv.at[2], tile_ss.at[2], tile_rs.at[2],
            device_id=(my_blk, across), device_id_type=MESH)

    def send_tiles():
        owner = tile_owner[...]
        group = owner // (4 * levs)
        row = (owner // 4) % levs * (4 * peers) + group * 4 + owner % 4
        ids = lax.broadcasted_iota(jnp.int32, (4 * peers * levs, blocks), 0)
        hot = jnp.where(ids == row, 1.0, 0.0).astype(BF16)
        tiles[...] = split_dot(hot, grad[...]).reshape(levs, 4 * peers, cells)
        for copy in pair_copies():
            copy.start()

    def own_copy(off, whose):
        return pltpu.make_async_remote_copy(
            owned.at[peer_at(off)], owned_recv.at[whose], own_ss.at[off], own_rs.at[off],
            device_id=(peer_at(off), my_lev), device_id_type=MESH)

    def split_rows(value, target):
        width = value.shape[1]
        if cap % 8 == 0:
            target[...] = value.reshape(peers, cap, width)
        else:
            flat[:, :width] = value
            for p in range(peers):
                target[p] = flat[p * cap : (p + 1) * cap, :width]

    def join_rows(source):
        width = source.shape[-1]
        if cap % 8 == 0:
            return source[...].reshape(slots, width)
        for p in range(peers):
            flat[p * cap : (p + 1) * cap, :width] = source[p]
        return flat[:, :width]

    def prepare_routes():
        eye = (
            lax.broadcasted_iota(jnp.int32, (blocks, blocks), 0)
            == lax.broadcasted_iota(jnp.int32, (blocks, blocks), 1)
        )

        def column(row):
            return jnp.sum(jnp.where(eye, row, 0.0), axis=1, keepdims=True)

        dest = dest_device[...].astype(F32)
        same = jnp.logical_and(
            column(dest) == dest,
            lax.broadcasted_iota(jnp.int32, (blocks, blocks), 0)
            < lax.broadcasted_iota(jnp.int32, (blocks, blocks), 1),
        )
        rank = jnp.sum(jnp.where(same, 1.0, 0.0), axis=0, keepdims=True)
        slot_row = dest * cap + rank
        slot_id = lax.broadcasted_iota(jnp.int32, (slots, blocks), 0).astype(F32)
        pick[...] = jnp.where(slot_id == slot_row, 1.0, 0.0).astype(BF16)
        keys = column(dest_slot[...].astype(F32)) + jnp.zeros((blocks, 128), F32)
        split_rows(
            jnp.dot(pick[...], keys.astype(BF16), preferred_element_type=F32), key_send)
        key_recv[my_blk] = key_send[my_blk]
        each(peers, lambda off: key_copy(off, my_blk).start())

        face = lax.broadcasted_iota(jnp.int32, (cycle, cells), 0)
        cell = lax.broadcasted_iota(jnp.int32, (cycle, cells), 1)
        wanted = jnp.where(
            face < side, face,
            jnp.where(
                face < 2 * side, face + (cells - 2 * side),
                jnp.where(
                    face < 3 * side, (face - 2 * side) * side,
                    (face - 3 * side) * side + side - 1)))
        spread_t[...] = jnp.where(cell == wanted, 1.0, 0.0).astype(BF16)
        face = lax.broadcasted_iota(jnp.int32, (cells, cycle), 1)
        cell = lax.broadcasted_iota(jnp.int32, (cells, cycle), 0)
        wanted = jnp.where(
            face < side, face,
            jnp.where(
                face < 2 * side, face + (cells - 2 * side),
                jnp.where(
                    face < 3 * side, (face - 2 * side) * side,
                    (face - 3 * side) * side + side - 1)))
        gather_t[...] = jnp.where(cell == wanted, 1.0, 0.0).astype(BF16)

        sub_wide[...] = column(substeps[...].astype(F32)) + jnp.zeros((blocks, 128), F32)

    def prepare_stencil():
        fetch.wait()

        @pl.loop(0, blocks // GROUP)
        def _(item):
            rows = pl.ds(pl.multiple_of(item * GROUP, GROUP), GROUP)
            cell = lax.broadcasted_iota(jnp.int32, (GROUP, cells), 1)
            total = jnp.zeros((GROUP, cells), F32)
            for level in range(lev_here):
                e, n = courant_here[0, level, rows, :], courant_here[1, level, rows, :]
                centre[level, rows, :] = 1.0 - e - n
                east[level, rows, :] = jnp.where((cell & (side - 1)) == side - 1, 0.0, e)
                north[level, rows, :] = jnp.where(cell >= cells - side, 0.0, n)
                total = total + profile[level] * adj[level, rows, :]
            grad[rows, :] = total


    def solve(step):
        @pl.when(outer)
        def _():
            for part in range(CHUNKS):
                @pl.loop(0, items)
                def _(item):
                    rows, own = rows_of(part, item), send_rows(item)
                    d, f = forward(
                        step, rows, jnp.ones((GROUP, cells), F32),
                        x[level_at(0), rows, :] * surv[level_at(0), rows, :])
                    if step == 0:
                        inv, c = link_pair(d, mix[last, rows, :], lower)
                        coef[end_c, rows, :] = c
                        coef[end_i, rows, :] = inv
                        line_send[STEPS, part, own, :] = c * d
                    else:
                        c = coef[end_c, rows, :]
                    line_send[step, part, own, :] = c * f

                if step == 0:
                    first_line(part, partner).start()
                line_copy(step, part, partner).start()
            if step == 0:
                prepare_routes()
                prepare_stencil()
            else:
                send_tiles()
            for part in range(CHUNKS):
                back_copy(step, part, partner).wait_recv()

                @pl.loop(0, items)
                def _(item):
                    rows, own = rows_of(part, item), send_rows(item)
                    value = x[level_at(last), rows, :] * coef[end_i, rows, :]
                    value = value + coef[end_c, rows, :] * back_recv[step, part, own, :]
                    backward(rows, value)

        @pl.when(jnp.logical_not(outer))
        def _():
            if step == 0:
                prepare_routes()
            for part in range(CHUNKS):
                if step == 0:
                    first_line(part, partner).wait_recv()
                line_copy(step, part, partner).wait_recv()

                @pl.loop(0, items)
                def _(item):
                    rows, own = rows_of(part, item), send_rows(item)
                    f_in = line_recv[step, part, own, :]
                    d = None
                    if step == 0:
                        d_in = line_recv[STEPS, part, own, :]
                        inv, c_in = link_pair(
                            d_in, mix[last, rows, :], jnp.logical_not(lower))
                        middle[0, rows, :] = inv
                        middle[1, rows, :] = c_in
                        d = 1.0 + c_in * d_in
                    else:
                        c_in = middle[1, rows, :]
                    d, f = forward(
                        step, rows, d,
                        x[level_at(0), rows, :] * surv[level_at(0), rows, :] + c_in * f_in)
                    if step == 0:
                        _, c = link_pair(d, mix[last, rows, :], lower)
                        coef[end_c, rows, :] = c
                        coef[end_i, rows, :] = d
                        cross_send[STEPS, part, own, :] = c * d
                    else:
                        c = coef[end_c, rows, :]
                    cross_send[step, part, own, :] = c * f

                if step == 0:
                    cross_copy(STEPS, part, across).start()
                cross_copy(step, part, across).start()
            if step == 0:
                prepare_stencil()
            else:
                send_tiles()
            for part in range(CHUNKS):
                if step == 0:
                    cross_copy(STEPS, part, across).wait_recv()
                cross_copy(step, part, across).wait_recv()

                @pl.loop(0, items)
                def _(item):
                    rows, own = rows_of(part, item), send_rows(item)
                    if step == 0:
                        d_in = cross_recv[STEPS, part, own, :]
                        _, c_in = link_pair(d_in, mix[last, rows, :], lower)
                        inv = 1.0 / (coef[end_i, rows, :] + c_in * d_in)
                        middle[2, rows, :] = c_in
                        middle[3, rows, :] = inv
                    else:
                        c_in = middle[2, rows, :]
                        inv = middle[3, rows, :]
                    value = (x[level_at(last), rows, :] + c_in * cross_recv[step, part, own, :]) * inv
                    value = backward(rows, value)
                    back_send[step, part, own, :] = (
                        middle[0, rows, :] * line_recv[step, part, own, :]
                        + middle[1, rows, :] * value)

                back_copy(step, part, partner).start()

    def finish_solve(step):
        @pl.when(outer)
        def _():
            for part in range(CHUNKS):
                if step == 0:
                    first_line(part, partner).wait_send()
                line_copy(step, part, partner).wait_send()

        @pl.when(jnp.logical_not(outer))
        def _():
            for part in range(CHUNKS):
                if step == 0:
                    cross_copy(STEPS, part, across).wait_send()
                cross_copy(step, part, across).wait_send()
                back_copy(step, part, partner).wait_send()

    for load in loads[:-1]:
        load.wait()

    @pl.loop(0, blocks // GROUP)
    def _(item):
        rows = pl.ds(pl.multiple_of(item * GROUP, GROUP), GROUP)
        for level in range(lev_here):
            surv[level, rows, :] = jnp.exp(-oh[level, rows, :])
            x[level, rows, :] = adj[level, rows, :]

    pl.semaphore_wait(barrier, peers - 1 + levs - 1)

    for step in range(STEPS):
        solve(step)
        cyc = split_dot(
            jnp.concatenate([x[level] for level in range(lev_here)], axis=0), gather_t[...])
        cyc = jnp.concatenate(
            [cyc[level * blocks : (level + 1) * blocks] * weight[...] for level in range(lev_here)],
            axis=1)
        split_rows(split_dot(pick[...], cyc), face_send.at[step])
        face_recv[step, my_blk] = face_send[step, my_blk]
        each(peers, lambda off: face_copy(step, off, my_blk).start())

        if step == STEPS - 1:
            for copy in pair_copies():
                copy.wait_send()
                copy.wait_recv()
            tiles[across] = tiles[across] + tiles_recv[1]
            far_copy().start()

        active = sub_wide[:, 0:1]

        @pl.loop(0, lev_here)
        def _(level):
            value = x[level]
            for substep in range(RMAX):
                moved = (
                    centre[level] * value
                    + east[level] * pltpu.roll(value, cells - 1, 1)
                    + north[level] * pltpu.roll(value, cells - side, 1))
                value = jnp.where(active > substep, moved, value)
            x[level] = value

        if step == 0:
            each(peers, lambda off: key_copy(off, source_at(off)).wait_recv())
            keys = join_rows(key_recv)
            lane = lax.broadcasted_iota(jnp.int32, (slots, 128), 1).astype(F32)
            place[...] = jnp.where(keys == lane, 1.0, 0.0).T[:blocks].astype(BF16)
        else:
            far_copy().wait_recv()
            total = tiles[my_lev] + tiles_recv[0] + tiles_recv[2]
            for p in range(peers):
                owned[p] = total[4 * p : 4 * p + 4]
            each(peers, lambda off: own_copy(off, my_blk).start())
        each(peers, lambda off: face_copy(step, off, source_at(off)).wait_recv())
        arrived = split_dot(place[...], join_rows(face_recv.at[step]))
        spread = split_dot(
            jnp.concatenate(
                [arrived[:, level * cycle : (level + 1) * cycle] for level in range(lev_here)],
                axis=0),
            spread_t[...])
        for level in range(lev_here):
            value = x[level] + spread[level * blocks : (level + 1) * blocks]
            if step < STEPS - 1:
                x[level] = value
                grad[...] = grad[...] + profile[level] * value
            else:
                x[level] = value
                pltpu.make_async_copy(x.at[level], out.at[level], store_sems.at[level]).start()

    each(peers, lambda off: own_copy(off, source_at(off)).wait_recv())
    tile_out[...] = owned[my_blk]

    def add_owned(off):
        tile_out[...] = tile_out[...] + owned_recv[source_at(off)]

    each(peers, add_owned)
    for level in range(lev_here):
        pltpu.make_async_copy(x.at[level], out.at[level], store_sems.at[level]).wait()
    for step in range(STEPS):
        finish_solve(step)
        each(peers, lambda off: face_copy(step, off, my_blk).wait_send())
    each(peers, lambda off: key_copy(off, my_blk).wait_send())
    far_copy().wait_send()
    each(peers, lambda off: own_copy(off, my_blk).wait_send())


def emit(field, tile_rows, out, tile_out):
    out[...] = field[...]
    tile_out[...] = tile_rows[...]


def local(
    adjoint_in,
    courant,
    mixing,
    oh_rate,
    substeps,
    nest_weight,
    dest_device,
    dest_slot,
    emission_profile,
    tile_owner,
):
    blocks, lev_here, cells = adjoint_in.shape
    cycle = nest_weight.shape[1]
    peers = lax.axis_size("blk")
    levs = lax.axis_size("lev")
    cap = min(blocks, 2 * blocks // peers)
    chunk = blocks // CHUNKS
    vmem = pl.BlockSpec(memory_space=pltpu.VMEM)
    whole = pltpu.VMEM((lev_here, blocks, cells), F32)
    line = pltpu.VMEM((STEPS + 1, CHUNKS, chunk, cells), F32)
    dma = pltpu.SemaphoreType.DMA
    out, tile_grad = pl.pallas_call(
        functools.partial(kernel, peers, levs),
        out_shape=(
            jax.ShapeDtypeStruct((lev_here, blocks, cells), F32),
            jax.ShapeDtypeStruct((4, cells), F32),
        ),
        in_specs=[pl.BlockSpec(memory_space=pl.ANY)] * 4 + [vmem] * 5
        + [pl.BlockSpec(memory_space=pltpu.SMEM)],
        out_specs=(pl.BlockSpec(memory_space=pl.ANY), vmem),
        scratch_shapes=[
            whole,
            whole,
            whole,
            whole,
            pltpu.VMEM((2, lev_here, blocks, cells), F32),
            dma((4,)),
            dma((lev_here,)),
            pltpu.VMEM((blocks, 128), F32),
            whole,
            whole,
            whole,
            whole,
            pltpu.VMEM((2 * lev_here, blocks, cells), F32),
            pltpu.VMEM((4, blocks, cells), F32),
            pltpu.VMEM((blocks, cells), F32),
            pltpu.VMEM((cells, cycle), BF16),
            pltpu.VMEM((cycle, cells), BF16),
            pltpu.VMEM((peers * cap, blocks), BF16),
            pltpu.VMEM((blocks, peers * cap), BF16),
            pltpu.VMEM((peers * cap, lev_here * cycle), F32),
            pltpu.VMEM((peers, cap, 128), F32),
            pltpu.VMEM((peers, cap, 128), F32),
            pltpu.VMEM((STEPS, peers, cap, lev_here * cycle), F32),
            pltpu.VMEM((STEPS, peers, cap, lev_here * cycle), F32),
            line,
            line,
            line,
            line,
            line,
            line,
            pltpu.VMEM((levs, 4 * peers, cells), F32),
            pltpu.VMEM((3, 4 * peers, cells), F32),
            pltpu.VMEM((peers, 4, cells), F32),
            pltpu.VMEM((peers, 4, cells), F32),
            dma((STEPS + 1, CHUNKS)),
            dma((STEPS + 1, CHUNKS)),
            dma((STEPS + 1, CHUNKS)),
            dma((STEPS + 1, CHUNKS)),
            dma((STEPS, CHUNKS)),
            dma((STEPS, CHUNKS)),
            dma((peers,)),
            dma((peers,)),
            dma((STEPS, peers)),
            dma((STEPS, peers)),
            dma((levs,)),
            dma((levs,)),
            dma((peers,)),
            dma((peers,)),
        ],
        compiler_params=pltpu.CompilerParams(
            collective_id=0, has_side_effects=True, vmem_limit_bytes=60 * 1024 * 1024
        ),
    )(
        jnp.transpose(adjoint_in, (1, 0, 2)),
        jnp.transpose(courant, (0, 2, 1, 3)),
        jnp.transpose(mixing, (1, 0, 2)),
        jnp.transpose(oh_rate, (1, 0, 2)),
        substeps.reshape(1, blocks),
        dest_device.reshape(1, blocks),
        dest_slot.reshape(1, blocks),
        tile_owner.reshape(1, blocks),
        nest_weight,
        emission_profile,
    )
    out, tile_grad = pl.pallas_call(
        emit,
        out_shape=(
            jax.ShapeDtypeStruct(out.shape, F32),
            jax.ShapeDtypeStruct(tile_grad.shape, F32),
        ),
        in_specs=[vmem, vmem],
        out_specs=(vmem, vmem),
    )(out, tile_grad)
    return jnp.transpose(out, (1, 0, 2)), tile_grad


def solution(mesh):
    placed = (
        P("blk", "lev", None),
        P(None, "blk", "lev", None),
        P("blk", "lev", None),
        P("blk", "lev", None),
        P("blk"),
        P("blk", None),
        P("blk", None),
        P("blk"),
        P("lev"),
        P("blk"),
    )
    return jax.shard_map(
        local,
        mesh=mesh,
        in_specs=placed,
        out_specs=(P("blk", "lev", None), P(("blk", "lev"), None)),
        check_vma=False,
    )
```

```python
import functools

import jax
import jax.numpy as jnp
from jax import lax
from jax.experimental import pallas as pl
from jax.experimental.pallas import tpu as pltpu
from jax.sharding import PartitionSpec as P

RMAX = 4
STEPS = 2
CHUNKS = 4
GROUP = 16
MESH = pl.DeviceIdType.MESH
F32 = jnp.float32
BF16 = jnp.bfloat16


def split_dot(left, right, dims=((1,), (0,))):
    def run(a, b):
        return lax.dot_general(a, b, (dims, ((), ())), preferred_element_type=F32)

    if left.dtype == BF16:
        high = right.astype(BF16)
        low = (right - high.astype(F32)).astype(BF16)
        return run(left, high) + run(left, low)
    rows = left.shape[0]
    high = left.astype(BF16)
    low = (left - high.astype(F32)).astype(BF16)
    both = run(jnp.concatenate([high, low], axis=0), right)
    return both[:rows] + both[rows:]


def each(count, body):
    if count <= 16:
        for off in range(1, count):
            body(off)
    else:
        lax.fori_loop(1, count, lambda off, c: (body(off), c)[1], 0)


def kernel(
    peers,
    levs,
    adj_far,
    courant,
    mix_far,
    oh_far,
    substeps,
    dest_device,
    dest_slot,
    tile_owner,
    weight,
    profile,
    out,
    tile_out,
    surv,
    adj,
    mix,
    oh,
    courant_here,
    load_sems,
    store_sems,
    sub_wide,
    centre,
    east,
    north,
    x,
    coef,
    middle,
    grad,
    gather_t,
    spread_t,
    pick,
    place,
    flat,
    key_send,
    key_recv,
    face_send,
    face_recv,
    line_send,
    line_recv,
    cross_send,
    cross_recv,
    back_send,
    back_recv,
    tiles,
    tiles_recv,
    owned,
    owned_recv,
    line_ss,
    line_rs,
    cross_ss,
    cross_rs,
    back_ss,
    back_rs,
    key_ss,
    key_rs,
    face_ss,
    face_rs,
    tile_ss,
    tile_rs,
    own_ss,
    own_rs,
):
    lev_here, blocks, cells = adj_far.shape
    cycle = weight.shape[1]
    side = cycle // 4
    cap = key_send.shape[1]
    slots = peers * cap
    chunk = blocks // CHUNKS
    my_blk = lax.axis_index("blk")
    my_lev = lax.axis_index("lev")
    lower = my_lev < 2
    outer = jnp.logical_or(my_lev == 0, my_lev == levs - 1)

    def peer_at(off):
        return lax.rem(my_blk + off, peers)

    def source_at(off):
        return lax.rem(my_blk + peers - off, peers)

    loads = [
        pltpu.make_async_copy(source, target, load_sems.at[n])
        for n, (source, target) in enumerate(
            [(oh_far, oh), (adj_far, adj), (mix_far, mix), (courant, courant_here)])
    ]
    fetch = loads[-1]
    for load in loads:
        load.start()
    barrier = pltpu.get_barrier_semaphore()
    each(peers, lambda off: pl.semaphore_signal(
        barrier, inc=1, device_id=(peer_at(off), my_lev), device_id_type=MESH))
    for off in range(1, levs):
        pl.semaphore_signal(
            barrier, inc=1, device_id=(my_blk, lax.rem(my_lev + off, levs)), device_id_type=MESH)

    def rows_of(part, item):
        return pl.ds(pl.multiple_of(part * chunk + item * GROUP, GROUP), GROUP)

    def level_at(p):
        return jnp.where(lower, p, lev_here - 1 - p)

    def link_at(p):
        return jnp.where(lower, p, lev_here - 2 - p)

    def link_pair(d, k, flag):
        inv = 1.0 / (d + k)
        return jnp.where(flag, inv, 0.0), jnp.where(flag, k * inv, 1.0)

    last = lev_here - 1

    def line_copy(step, part, target):
        return pltpu.make_async_remote_copy(
            line_send.at[step, part], line_recv.at[step, part],
            line_ss.at[step, part], line_rs.at[step, part],
            device_id=(my_blk, target), device_id_type=MESH)

    def first_line(part, target):
        return pltpu.make_async_remote_copy(
            line_send.at[STEPS, part], line_recv.at[STEPS, part],
            line_ss.at[STEPS, part], line_rs.at[STEPS, part],
            device_id=(my_blk, target), device_id_type=MESH)

    def cross_copy(step, part, target):
        return pltpu.make_async_remote_copy(
            cross_send.at[step, part], cross_recv.at[step, part],
            cross_ss.at[step, part], cross_rs.at[step, part],
            device_id=(my_blk, target), device_id_type=MESH)

    def back_copy(step, part, target):
        return pltpu.make_async_remote_copy(
            back_send.at[step, part], back_recv.at[step, part],
            back_ss.at[step, part], back_rs.at[step, part],
            device_id=(my_blk, target), device_id_type=MESH)

    partner = jnp.where(lower, 1 - my_lev, 5 - my_lev)
    across = 3 - my_lev

    def forward(step, rows, d, f):
        for p in range(lev_here):
            if p > 0:
                c = coef[2 * (p - 1), rows, :]
                f = x[level_at(p), rows, :] * surv[level_at(p), rows, :] + c * f
            x[level_at(p), rows, :] = f
            if step == 0:
                if p > 0:
                    d = 1.0 + c * d
                if p < last:
                    k = mix[link_at(p), rows, :]
                    inv = 1.0 / (d + k)
                    coef[2 * p, rows, :] = k * inv
                    coef[2 * p + 1, rows, :] = inv
        return d, f

    def backward(rows, value):
        x[level_at(last), rows, :] = value
        for p in range(last - 1, -1, -1):
            value = x[level_at(p), rows, :] * coef[2 * p + 1, rows, :] + coef[2 * p, rows, :] * value
            x[level_at(p), rows, :] = value
        return value

    items = chunk // GROUP
    end_c, end_i = 2 * last, 2 * last + 1

    def send_rows(item):
        return pl.ds(pl.multiple_of(item * GROUP, GROUP), GROUP)

    def key_copy(off, whose):
        return pltpu.make_async_remote_copy(
            key_send.at[peer_at(off)], key_recv.at[whose], key_ss.at[off], key_rs.at[off],
            device_id=(peer_at(off), my_lev), device_id_type=MESH)

    def face_copy(step, off, whose):
        return pltpu.make_async_remote_copy(
            face_send.at[step, peer_at(off)], face_recv.at[step, whose],
            face_ss.at[step, off], face_rs.at[step, off],
            device_id=(peer_at(off), my_lev), device_id_type=MESH)

    def pair_copy(which, target):
        return pltpu.make_async_remote_copy(
            tiles.at[target], tiles_recv.at[which], tile_ss.at[which], tile_rs.at[which],
            device_id=(my_blk, partner), device_id_type=MESH)

    def pair_copies():
        return [pair_copy(0, partner), pair_copy(1, levs - 1 - partner)]

    def far_copy():
        return pltpu.make_async_remote_copy(
            tiles.at[across], tiles_recv.at[2], tile_ss.at[2], tile_rs.at[2],
            device_id=(my_blk, across), device_id_type=MESH)

    def send_tiles():
        owner = tile_owner[...]
        group = owner // (4 * levs)
        row = (owner // 4) % levs * (4 * peers) + group * 4 + owner % 4
        ids = lax.broadcasted_iota(jnp.int32, (4 * peers * levs, blocks), 0)
        hot = jnp.where(ids == row, 1.0, 0.0).astype(BF16)
        tiles[...] = split_dot(hot, grad[...]).reshape(levs, 4 * peers, cells)
        for copy in pair_copies():
            copy.start()

    def own_copy(off, whose):
        return pltpu.make_async_remote_copy(
            owned.at[peer_at(off)], owned_recv.at[whose], own_ss.at[off], own_rs.at[off],
            device_id=(peer_at(off), my_lev), device_id_type=MESH)

    def split_rows(value, target):
        width = value.shape[1]
        if cap % 8 == 0:
            target[...] = value.reshape(peers, cap, width)
        else:
            flat[:, :width] = value
            for p in range(peers):
                target[p] = flat[p * cap : (p + 1) * cap, :width]

    def join_rows(source):
        width = source.shape[-1]
        if cap % 8 == 0:
            return source[...].reshape(slots, width)
        for p in range(peers):
            flat[p * cap : (p + 1) * cap, :width] = source[p]
        return flat[:, :width]

    def prepare_routes():
        eye = (
            lax.broadcasted_iota(jnp.int32, (blocks, blocks), 0)
            == lax.broadcasted_iota(jnp.int32, (blocks, blocks), 1)
        )

        def column(row):
            return jnp.sum(jnp.where(eye, row, 0.0), axis=1, keepdims=True)

        dest = dest_device[...].astype(F32)
        same = jnp.logical_and(
            column(dest) == dest,
            lax.broadcasted_iota(jnp.int32, (blocks, blocks), 0)
            < lax.broadcasted_iota(jnp.int32, (blocks, blocks), 1),
        )
        rank = jnp.sum(jnp.where(same, 1.0, 0.0), axis=0, keepdims=True)
        slot_row = dest * cap + rank
        slot_id = lax.broadcasted_iota(jnp.int32, (slots, blocks), 0).astype(F32)
        pick[...] = jnp.where(slot_id == slot_row, 1.0, 0.0).astype(BF16)
        keys = column(dest_slot[...].astype(F32)) + jnp.zeros((blocks, 128), F32)
        split_rows(
            jnp.dot(pick[...], keys.astype(BF16), preferred_element_type=F32), key_send)
        key_recv[my_blk] = key_send[my_blk]
        each(peers, lambda off: key_copy(off, my_blk).start())

        face = lax.broadcasted_iota(jnp.int32, (cycle, cells), 0)
        cell = lax.broadcasted_iota(jnp.int32, (cycle, cells), 1)
        wanted = jnp.where(
            face < side, face,
            jnp.where(
                face < 2 * side, face + (cells - 2 * side),
                jnp.where(
                    face < 3 * side, (face - 2 * side) * side,
                    (face - 3 * side) * side + side - 1)))
        spread_t[...] = jnp.where(cell == wanted, 1.0, 0.0).astype(BF16)
        face = lax.broadcasted_iota(jnp.int32, (cells, cycle), 1)
        cell = lax.broadcasted_iota(jnp.int32, (cells, cycle), 0)
        wanted = jnp.where(
            face < side, face,
            jnp.where(
                face < 2 * side, face + (cells - 2 * side),
                jnp.where(
                    face < 3 * side, (face - 2 * side) * side,
                    (face - 3 * side) * side + side - 1)))
        gather_t[...] = jnp.where(cell == wanted, 1.0, 0.0).astype(BF16)

        sub_wide[...] = column(substeps[...].astype(F32)) + jnp.zeros((blocks, 128), F32)

    def prepare_stencil():
        fetch.wait()

        @pl.loop(0, blocks // GROUP)
        def _(item):
            rows = pl.ds(pl.multiple_of(item * GROUP, GROUP), GROUP)
            cell = lax.broadcasted_iota(jnp.int32, (GROUP, cells), 1)
            total = jnp.zeros((GROUP, cells), F32)
            for level in range(lev_here):
                e, n = courant_here[0, level, rows, :], courant_here[1, level, rows, :]
                centre[level, rows, :] = 1.0 - e - n
                east[level, rows, :] = jnp.where((cell & (side - 1)) == side - 1, 0.0, e)
                north[level, rows, :] = jnp.where(cell >= cells - side, 0.0, n)
                total = total + profile[level] * adj[level, rows, :]
            grad[rows, :] = total


    def solve(step):
        @pl.when(outer)
        def _():
            for part in range(CHUNKS):
                @pl.loop(0, items)
                def _(item):
                    rows, own = rows_of(part, item), send_rows(item)
                    d, f = forward(
                        step, rows, jnp.ones((GROUP, cells), F32),
                        x[level_at(0), rows, :] * surv[level_at(0), rows, :])
                    if step == 0:
                        inv, c = link_pair(d, mix[last, rows, :], lower)
                        coef[end_c, rows, :] = c
                        coef[end_i, rows, :] = inv
                        line_send[STEPS, part, own, :] = c * d
                    else:
                        c = coef[end_c, rows, :]
                    line_send[step, part, own, :] = c * f

                if step == 0:
                    first_line(part, partner).start()
                line_copy(step, part, partner).start()
            if step == 0:
                prepare_routes()
                prepare_stencil()
            else:
                send_tiles()
            for part in range(CHUNKS):
                back_copy(step, part, partner).wait_recv()

                @pl.loop(0, items)
                def _(item):
                    rows, own = rows_of(part, item), send_rows(item)
                    value = x[level_at(last), rows, :] * coef[end_i, rows, :]
                    value = value + coef[end_c, rows, :] * back_recv[step, part, own, :]
                    backward(rows, value)

        @pl.when(jnp.logical_not(outer))
        def _():
            if step == 0:
                prepare_routes()
            for part in range(CHUNKS):
                if step == 0:
                    first_line(part, partner).wait_recv()
                line_copy(step, part, partner).wait_recv()

                @pl.loop(0, items)
                def _(item):
                    rows, own = rows_of(part, item), send_rows(item)
                    f_in = line_recv[step, part, own, :]
                    d = None
                    if step == 0:
                        d_in = line_recv[STEPS, part, own, :]
                        inv, c_in = link_pair(
                            d_in, mix[last, rows, :], jnp.logical_not(lower))
                        middle[0, rows, :] = inv
                        middle[1, rows, :] = c_in
                        d = 1.0 + c_in * d_in
                    else:
                        c_in = middle[1, rows, :]
                    d, f = forward(
                        step, rows, d,
                        x[level_at(0), rows, :] * surv[level_at(0), rows, :] + c_in * f_in)
                    if step == 0:
                        _, c = link_pair(d, mix[last, rows, :], lower)
                        coef[end_c, rows, :] = c
                        coef[end_i, rows, :] = d
                        cross_send[STEPS, part, own, :] = c * d
                    else:
                        c = coef[end_c, rows, :]
                    cross_send[step, part, own, :] = c * f

                if step == 0:
                    cross_copy(STEPS, part, across).start()
                cross_copy(step, part, across).start()
            if step == 0:
                prepare_stencil()
            else:
                send_tiles()
            for part in range(CHUNKS):
                if step == 0:
                    cross_copy(STEPS, part, across).wait_recv()
                cross_copy(step, part, across).wait_recv()

                @pl.loop(0, items)
                def _(item):
                    rows, own = rows_of(part, item), send_rows(item)
                    if step == 0:
                        d_in = cross_recv[STEPS, part, own, :]
                        _, c_in = link_pair(d_in, mix[last, rows, :], lower)
                        inv = 1.0 / (coef[end_i, rows, :] + c_in * d_in)
                        middle[2, rows, :] = c_in
                        middle[3, rows, :] = inv
                    else:
                        c_in = middle[2, rows, :]
                        inv = middle[3, rows, :]
                    value = (x[level_at(last), rows, :] + c_in * cross_recv[step, part, own, :]) * inv
                    value = backward(rows, value)
                    back_send[step, part, own, :] = (
                        middle[0, rows, :] * line_recv[step, part, own, :]
                        + middle[1, rows, :] * value)

                back_copy(step, part, partner).start()

    def finish_solve(step):
        @pl.when(outer)
        def _():
            for part in range(CHUNKS):
                if step == 0:
                    first_line(part, partner).wait_send()
                line_copy(step, part, partner).wait_send()

        @pl.when(jnp.logical_not(outer))
        def _():
            for part in range(CHUNKS):
                if step == 0:
                    cross_copy(STEPS, part, across).wait_send()
                cross_copy(step, part, across).wait_send()
                back_copy(step, part, partner).wait_send()

    for load in loads[:-1]:
        load.wait()

    @pl.loop(0, blocks // GROUP)
    def _(item):
        rows = pl.ds(pl.multiple_of(item * GROUP, GROUP), GROUP)
        for level in range(lev_here):
            surv[level, rows, :] = jnp.exp(-oh[level, rows, :])
            x[level, rows, :] = adj[level, rows, :]

    pl.semaphore_wait(barrier, peers - 1 + levs - 1)

    for step in range(STEPS):
        solve(step)
        if step == STEPS - 1:
            for copy in pair_copies():
                copy.wait_send()
                copy.wait_recv()
            tiles[across] = tiles[across] + tiles_recv[1]
            far_copy().start()

        cyc = split_dot(
            jnp.concatenate([x[level] for level in range(lev_here)], axis=0), gather_t[...])
        cyc = jnp.concatenate(
            [cyc[level * blocks : (level + 1) * blocks] * weight[...] for level in range(lev_here)],
            axis=1)
        split_rows(split_dot(pick[...], cyc), face_send.at[step])
        face_recv[step, my_blk] = face_send[step, my_blk]
        each(peers, lambda off: face_copy(step, off, my_blk).start())

        active = sub_wide[:, 0:1]

        @pl.loop(0, lev_here)
        def _(level):
            value = x[level]
            for substep in range(RMAX):
                moved = (
                    centre[level] * value
                    + east[level] * pltpu.roll(value, cells - 1, 1)
                    + north[level] * pltpu.roll(value, cells - side, 1))
                value = jnp.where(active > substep, moved, value)
            x[level] = value

        if step == 0:
            each(peers, lambda off: key_copy(off, source_at(off)).wait_recv())
            keys = join_rows(key_recv)
            lane = lax.broadcasted_iota(jnp.int32, (slots, 128), 1).astype(F32)
            place[...] = jnp.where(keys == lane, 1.0, 0.0).T[:blocks].astype(BF16)
        else:
            far_copy().wait_recv()
            total = tiles[my_lev] + tiles_recv[0] + tiles_recv[2]
            for p in range(peers):
                owned[p] = total[4 * p : 4 * p + 4]
            each(peers, lambda off: own_copy(off, my_blk).start())
        each(peers, lambda off: face_copy(step, off, source_at(off)).wait_recv())
        arrived = split_dot(place[...], join_rows(face_recv.at[step]))
        spread = split_dot(
            jnp.concatenate(
                [arrived[:, level * cycle : (level + 1) * cycle] for level in range(lev_here)],
                axis=0),
            spread_t[...])
        for level in range(lev_here):
            value = x[level] + spread[level * blocks : (level + 1) * blocks]
            if step < STEPS - 1:
                x[level] = value
                grad[...] = grad[...] + profile[level] * value
            else:
                x[level] = value
                pltpu.make_async_copy(x.at[level], out.at[level], store_sems.at[level]).start()

    each(peers, lambda off: own_copy(off, source_at(off)).wait_recv())
    tile_out[...] = owned[my_blk]

    def add_owned(off):
        tile_out[...] = tile_out[...] + owned_recv[source_at(off)]

    each(peers, add_owned)
    for level in range(lev_here):
        pltpu.make_async_copy(x.at[level], out.at[level], store_sems.at[level]).wait()
    for step in range(STEPS):
        finish_solve(step)
        each(peers, lambda off: face_copy(step, off, my_blk).wait_send())
    each(peers, lambda off: key_copy(off, my_blk).wait_send())
    far_copy().wait_send()
    each(peers, lambda off: own_copy(off, my_blk).wait_send())


def emit(field, tile_rows, out, tile_out):
    out[...] = field[...]
    tile_out[...] = tile_rows[...]


def local(
    adjoint_in,
    courant,
    mixing,
    oh_rate,
    substeps,
    nest_weight,
    dest_device,
    dest_slot,
    emission_profile,
    tile_owner,
):
    blocks, lev_here, cells = adjoint_in.shape
    cycle = nest_weight.shape[1]
    peers = lax.axis_size("blk")
    levs = lax.axis_size("lev")
    cap = min(blocks, 2 * blocks // peers)
    chunk = blocks // CHUNKS
    vmem = pl.BlockSpec(memory_space=pltpu.VMEM)
    whole = pltpu.VMEM((lev_here, blocks, cells), F32)
    line = pltpu.VMEM((STEPS + 1, CHUNKS, chunk, cells), F32)
    dma = pltpu.SemaphoreType.DMA
    out, tile_grad = pl.pallas_call(
        functools.partial(kernel, peers, levs),
        out_shape=(
            jax.ShapeDtypeStruct((lev_here, blocks, cells), F32),
            jax.ShapeDtypeStruct((4, cells), F32),
        ),
        in_specs=[pl.BlockSpec(memory_space=pl.ANY)] * 4 + [vmem] * 5
        + [pl.BlockSpec(memory_space=pltpu.SMEM)],
        out_specs=(pl.BlockSpec(memory_space=pl.ANY), vmem),
        scratch_shapes=[
            whole,
            whole,
            whole,
            whole,
            pltpu.VMEM((2, lev_here, blocks, cells), F32),
            dma((4,)),
            dma((lev_here,)),
            pltpu.VMEM((blocks, 128), F32),
            whole,
            whole,
            whole,
            whole,
            pltpu.VMEM((2 * lev_here, blocks, cells), F32),
            pltpu.VMEM((4, blocks, cells), F32),
            pltpu.VMEM((blocks, cells), F32),
            pltpu.VMEM((cells, cycle), BF16),
            pltpu.VMEM((cycle, cells), BF16),
            pltpu.VMEM((peers * cap, blocks), BF16),
            pltpu.VMEM((blocks, peers * cap), BF16),
            pltpu.VMEM((peers * cap, lev_here * cycle), F32),
            pltpu.VMEM((peers, cap, 128), F32),
            pltpu.VMEM((peers, cap, 128), F32),
            pltpu.VMEM((STEPS, peers, cap, lev_here * cycle), F32),
            pltpu.VMEM((STEPS, peers, cap, lev_here * cycle), F32),
            line,
            line,
            line,
            line,
            line,
            line,
            pltpu.VMEM((levs, 4 * peers, cells), F32),
            pltpu.VMEM((3, 4 * peers, cells), F32),
            pltpu.VMEM((peers, 4, cells), F32),
            pltpu.VMEM((peers, 4, cells), F32),
            dma((STEPS + 1, CHUNKS)),
            dma((STEPS + 1, CHUNKS)),
            dma((STEPS + 1, CHUNKS)),
            dma((STEPS + 1, CHUNKS)),
            dma((STEPS, CHUNKS)),
            dma((STEPS, CHUNKS)),
            dma((peers,)),
            dma((peers,)),
            dma((STEPS, peers)),
            dma((STEPS, peers)),
            dma((levs,)),
            dma((levs,)),
            dma((peers,)),
            dma((peers,)),
        ],
        compiler_params=pltpu.CompilerParams(
            collective_id=0, has_side_effects=True, vmem_limit_bytes=60 * 1024 * 1024
        ),
    )(
        jnp.transpose(adjoint_in, (1, 0, 2)),
        jnp.transpose(courant, (0, 2, 1, 3)),
        jnp.transpose(mixing, (1, 0, 2)),
        jnp.transpose(oh_rate, (1, 0, 2)),
        substeps.reshape(1, blocks),
        dest_device.reshape(1, blocks),
        dest_slot.reshape(1, blocks),
        tile_owner.reshape(1, blocks),
        nest_weight,
        emission_profile,
    )
    out, tile_grad = pl.pallas_call(
        emit,
        out_shape=(
            jax.ShapeDtypeStruct(out.shape, F32),
            jax.ShapeDtypeStruct(tile_grad.shape, F32),
        ),
        in_specs=[vmem, vmem],
        out_specs=(vmem, vmem),
    )(out, tile_grad)
    return jnp.transpose(out, (1, 0, 2)), tile_grad


def solution(mesh):
    placed = (
        P("blk", "lev", None),
        P(None, "blk", "lev", None),
        P("blk", "lev", None),
        P("blk", "lev", None),
        P("blk"),
        P("blk", None),
        P("blk", None),
        P("blk"),
        P("lev"),
        P("blk"),
    )
    return jax.shard_map(
        local,
        mesh=mesh,
        in_specs=placed,
        out_specs=(P("blk", "lev", None), P(("blk", "lev"), None)),
        check_vma=False,
    )
```
